32 devices in a mesh: group: 2 (over x), lane: 16 (over z, y, core).
Axes of the slice: x: 2, y: 2, z: 4, core: 2. Of those that a mesh axis runs over, the one named last changes fastest.
Arguments:
- queries: bfloat16 [8, 768], replicated, may hold values from -6 to 6
- hyper_weight: bfloat16 [768, 589824], P(None, ('group', 'lane')), may hold values from -0.0078125 to 0.0078125
- hyper_bias: bfloat16 [768, 768], P(None, ('group', 'lane')), may hold values from -0.21875 to 0.21875
- documents: bfloat16 [16384, 768], P(('group', 'lane')), may hold values from -6 to 6
- teacher: bfloat16 [16384, 8], P(('group', 'lane')), may hold values from 8 to 24
Outputs:
- doc_grad: bfloat16 [16384, 768], P(('group', 'lane'))
- weight_grad: bfloat16 [768, 589824], P(None, ('group', 'lane'))
- bias_grad: bfloat16 [768, 768], P(None, ('group', 'lane'))
The draws below stay inside these ranges and needn't reach their ends.
All inputs are finite; a program needn't handle non-finite values.
Results may differ from the reference program's by a relative error of at most 0.024.
The reference program's roundings to bfloat16 on the way count: a program that leaves them out, or rounds other values in their place, can miss the bound.
Values may be sent and summed in bfloat16 or wider, within the bound.
A program may use at most 192 MiB of HBM per device.

```python
import jax
import jax.numpy as jnp
from jax import lax

D = 768
QUERIES = 8
DOCS = 16384


def level_of(rng, extent, split, least, top_value):
    def one(dim, shards_of):
        draws = jax.random.uniform(jax.random.fold_in(jax.random.fold_in(rng, 6), dim), (shards_of,), jnp.float32, least / len(split), top_value / len(split))
        return jnp.repeat(jnp.exp(draws), extent[dim] // shards_of).reshape((-1,) + (1,) * (len(extent) - dim - 1))

    factor_of = one(*split[0])
    for cut in split[1:]:
        factor_of = factor_of * one(*cut)
    return factor_of


def scatter_about(key, shape, spread, limit, split=(), held_as=jnp.bfloat16):
    level = level_of(key, shape, split, -0.22, 0.18) if split else 1.0
    drawn = jax.random.normal(key, shape, jnp.float32) * spread * level
    return jnp.minimum(jnp.maximum(drawn, -limit), limit).astype(held_as)


def setup_inputs(seed: int = 0) -> dict:
    key_of = jax.random.split(jax.random.key(seed), 6)
    return {
        "queries": scatter_about(key_of[0], (QUERIES, D), 1.0, 6.0),
        "hyper_weight": scatter_about(key_of[1], (D, D * D), (D * D) ** -0.5, 0.0078125, ((1, 32),)),
        "hyper_bias": scatter_about(key_of[2], (D, D), D ** -0.5, 0.21875, ((1, 32),)),
        "documents": scatter_about(key_of[3], (DOCS, D), 1.0, 6.0, ((0, 32),)),
        "teacher": jnp.clip(8.0 + 16.0 * jax.random.uniform(key_of[4], (DOCS, QUERIES), jnp.float32) ** level_of(key_of[4], (DOCS, QUERIES), ((0, 32),), -0.2, 0.2), 8.0, 24.0).astype(jnp.bfloat16),
    }


def reference(queries, hyper_weight, hyper_bias, documents, teacher):
    pool_scale = D ** -0.5
    query_count = queries.shape[0]
    generated = jnp.dot(queries, hyper_weight, preferred_element_type=jnp.float32).astype(jnp.bfloat16).reshape(query_count, D, D)
    gen_bias = jnp.dot(queries, hyper_bias, preferred_element_type=jnp.float32).astype(jnp.bfloat16)
    doc_float = documents.astype(jnp.float32)

    def one_query(doc_total, inputs):
        layer, bias, target = inputs
        layer_float = layer.astype(jnp.float32)
        preact = jnp.dot(doc_float, layer_float, precision=lax.Precision.HIGHEST) + bias.astype(jnp.float32)
        scores = jnp.sum(jnp.maximum(preact, 0.0), axis=1) * pool_scale
        errors = scores - target.astype(jnp.float32)
        back_pre = jnp.where(preact > 0, errors[:, None] * pool_scale, 0.0).astype(jnp.bfloat16)
        back_pre = lax.optimization_barrier(back_pre).astype(jnp.float32)
        layer_grad = jnp.dot(doc_float.T, back_pre, precision=lax.Precision.HIGHEST)
        bias_part = jnp.sum(back_pre, axis=0)
        doc_total = doc_total + jnp.dot(back_pre, layer_float.T, precision=lax.Precision.HIGHEST)
        return doc_total, (layer_grad, bias_part)

    doc_grad, (layer_grads, bias_parts) = lax.scan(one_query, jnp.zeros(doc_float.shape, jnp.float32), (generated, gen_bias, teacher.T))
    layer_grads = layer_grads.astype(jnp.bfloat16).reshape(query_count, D * D)
    bias_parts = bias_parts.astype(jnp.bfloat16)
    weight_grad = jnp.dot(queries.T, layer_grads, preferred_element_type=jnp.float32).astype(jnp.bfloat16)
    bias_grad = jnp.dot(queries.T, bias_parts, preferred_element_type=jnp.float32).astype(jnp.bfloat16)
    return doc_grad.astype(jnp.bfloat16), weight_grad, bias_grad
```

```python
import functools

import jax
import jax.numpy as jnp
from jax import lax
from jax.experimental import pallas as pl
from jax.experimental.pallas import tpu as pltpu
from jax.sharding import PartitionSpec as P

MESH = pl.DeviceIdType.MESH
MIB = 1024 * 1024


def window_kernel(
    depth,
    per_group,
    layer_rows,
    scale,
    docs_ref,
    docs_t_ref,
    layers_ref,
    bias_ref,
    target_ref,
    doc_out,
    grad_out,
    bias_out,
    back_ref,
    doc_acc,
    sums,
    send1,
    recv1,
    send2,
    recv2,
    send3,
    recv3,
    final,
    send4,
    recv4,
    doc_send,
    doc_recv,
    bias_send,
    bias_recv,
    s1,
    r1,
    s2,
    r2,
    s3,
    r3,
    sb,
    rb,
    sx,
    rx,
):
    group = lax.axis_index("group")
    lane = lax.axis_index("lane")
    core = lax.rem(lane, 2)
    y = lax.rem(lane // 2, 2)
    z = lane // 4
    chunk = 2 * layer_rows
    features = layers_ref.shape[1]
    doc_rows = docs_ref.shape[0]
    own_docs = doc_rows // 2
    to_core = (group, lane + 1 - 2 * core)
    to_y = (group, lane + 2 - 4 * y)
    to_x = (1 - group, lane)

    def z_peer(step):
        return lax.rem(z + step, depth)

    def to_z(step):
        return (group, z_peer(step) * 4 + y * 2 + core)

    peers = [to_core, to_y, to_x] + [to_z(step) for step in range(1, depth)]
    barrier = pltpu.get_barrier_semaphore()
    for peer in peers:
        pl.semaphore_signal(barrier, inc=1, device_id=peer, device_id_type=MESH)
    pl.semaphore_wait(barrier, len(peers))

    def remote(src, dst, send_sem, recv_sem, peer):
        return pltpu.make_async_remote_copy(
            src_ref=src,
            dst_ref=dst,
            send_sem=send_sem,
            recv_sem=recv_sem,
            device_id=peer,
            device_id_type=MESH,
        )

    def copy1(q):
        return remote(send1.at[q], recv1.at[q], s1.at[q], r1.at[q], to_core)

    def copy2(q):
        return remote(send2.at[q], recv2.at[q], s2.at[q], r2.at[q], to_y)

    def copy3(q, step):
        k = step - 1
        return remote(send3.at[q, k], recv3.at[q, k], s3.at[q, k], r3.at[q, k], to_z(step))

    def bias_copy(k, peer):
        slot = min(k, 2)
        return remote(bias_send.at[slot], bias_recv.at[k], sb.at[k], rb.at[k], peer)

    doc_copy = remote(doc_send, doc_recv, sx.at[0], rx.at[0], to_x)
    grad_copy = remote(send4, recv4, sx.at[1], rx.at[1], to_x)
    bias_x_copy = remote(bias_send.at[3], bias_recv.at[depth + 1], sx.at[2], rx.at[2], to_x)

    def stage2(q):
        copy1(q).wait_recv()

        def part(k, carry):
            mine, theirs = k * 2 + y, k * 2 + 1 - y
            sums[q, mine, core] = sums[q, mine, core] + recv1[q, mine].astype(jnp.float32)
            send2[q, k] = (
                sums[q, theirs, core] + recv1[q, theirs].astype(jnp.float32)
            ).astype(jnp.bfloat16)
            return carry

        lax.fori_loop(0, depth, part, 0)
        copy2(q).start()

    def stage3(q):
        copy2(q).wait_recv()
        for step in range(1, depth):
            to = z_peer(step)
            send3[q, step - 1] = (
                sums[q, to * 2 + y, core] + recv2[q, to].astype(jnp.float32)
            ).astype(jnp.bfloat16)
            copy3(q, step).start()
        sums[q, z * 2 + y, core] = sums[q, z * 2 + y, core] + recv2[q, z].astype(jnp.float32)

    def finish(q):
        total = sums[q, z * 2 + y, core]
        for step in range(1, depth):
            copy3(q, step).wait_recv()
            total = total + recv3[q, step - 1].astype(jnp.float32)
        final[q] = total.reshape(2, layer_rows, features)

    tile = doc_rows // 4 if doc_rows % 64 == 0 else doc_rows
    bias_send[0] = jnp.zeros(bias_send.shape[1:], jnp.float32)

    for q in range(per_group):

        def rows_of(c, bias_sum):
            rows = pl.ds(pl.multiple_of(c * tile, tile), tile)
            layer = layers_ref[q]
            preact = (
                jnp.dot(docs_ref[rows, :], layer, preferred_element_type=jnp.float32)
                + bias_ref[q : q + 1, :]
            )
            scores = jnp.sum(jnp.maximum(preact, 0.0), axis=1, keepdims=True) * scale
            errors = (scores - target_ref[rows, q : q + 1]) * scale
            back = jnp.where(preact > 0, errors, 0.0).astype(jnp.bfloat16)
            back_ref[rows, :] = back
            term = lax.dot_general(
                back, layer, (((1,), (1,)), ((), ())), preferred_element_type=jnp.float32
            )
            if q == 0:
                doc_acc[rows, :] = term
            else:
                doc_acc[rows, :] = doc_acc[rows, :] + term
            return bias_sum + jnp.sum(back.astype(jnp.float32), axis=0, keepdims=True)

        bias_send[0, q : q + 1, :] = lax.fori_loop(
            0, doc_rows // tile, rows_of, jnp.zeros((1, features), jnp.float32)
        )
        if q >= 1:
            stage2(q - 1)
        if q == per_group - 1:
            doc_send[...] = doc_acc[own_docs:, :].astype(jnp.bfloat16)
            doc_copy.start()
            bias_copy(0, to_core).start()

        def grad_rows(t, carry):
            size = depth * chunk
            rows = pl.ds(pl.multiple_of(t * size, size), size)
            block = jnp.dot(
                docs_t_ref[rows, :], back_ref[...], preferred_element_type=jnp.float32
            )
            first = pl.ds(t * (depth // 2), depth // 2)
            sums[q, first] = block.reshape(depth // 2, 2, chunk, features)
            send1[q, first] = sums[q, first, 1 - core].astype(jnp.bfloat16)
            return carry

        lax.fori_loop(0, 4, grad_rows, 0)
        copy1(q).start()
        if q >= 1:
            stage3(q - 1)

    bias_copy(0, to_core).wait_recv()
    bias_send[1] = bias_send[0] + bias_recv[0]
    bias_copy(1, to_y).start()
    stage2(per_group - 1)
    bias_copy(1, to_y).wait_recv()
    bias_send[2] = bias_send[1] + bias_recv[1]
    for step in range(1, depth):
        bias_copy(1 + step, to_z(step)).start()
    for q in range(per_group - 1):
        finish(q)
    bias_total = bias_send[2]
    for step in range(1, depth):
        bias_copy(1 + step, to_z(step)).wait_recv()
        bias_total = bias_total + bias_recv[1 + step]
    bias_send[3] = bias_total
    bias_x_copy.start()
    doc_copy.wait_recv()
    doc_out[...] = (doc_acc[:own_docs, :] + doc_recv[...].astype(jnp.float32)).astype(jnp.bfloat16)
    stage3(per_group - 1)
    finish(per_group - 1)
    send4[...] = final[:, 1 - group].reshape(send4.shape).astype(jnp.bfloat16)
    grad_copy.start()
    grad_out[group] = final[:, group].reshape(send4.shape).astype(jnp.bfloat16)
    bias_out[group] = bias_total
    bias_x_copy.wait_recv()
    bias_out[1 - group] = bias_recv[depth + 1]
    grad_copy.wait_recv()
    grad_out[1 - group] = recv4[...]

    for q in range(per_group):
        copy1(q).wait_send()
        copy2(q).wait_send()
        for step in range(1, depth):
            copy3(q, step).wait_send()
    bias_copy(0, to_core).wait_send()
    bias_copy(1, to_y).wait_send()
    for step in range(1, depth):
        bias_copy(1 + step, to_z(step)).wait_send()
    doc_copy.wait_send()
    grad_copy.wait_send()
    bias_x_copy.wait_send()


def window(docs, docs_t, layers, biases, targets, depth, layer_rows, scale):
    per_group, features, _ = layers.shape
    doc_rows = docs.shape[0]
    chunk = 2 * layer_rows
    pairs = depth * 2
    bf16, f32 = jnp.bfloat16, jnp.float32
    vmem = pl.BlockSpec(memory_space=pltpu.VMEM)
    dma = pltpu.SemaphoreType.DMA
    flops = 6 * doc_rows * features * features * per_group
    return pl.pallas_call(
        functools.partial(window_kernel, depth, per_group, layer_rows, scale),
        out_shape=(
            jax.ShapeDtypeStruct((doc_rows // 2, features), bf16),
            jax.ShapeDtypeStruct((2, per_group * layer_rows, features), bf16),
            jax.ShapeDtypeStruct((2,) + biases.shape, f32),
        ),
        in_specs=[vmem] * 5,
        out_specs=(vmem, vmem, vmem),
        scratch_shapes=[
            pltpu.VMEM((doc_rows, features), bf16),
            pltpu.VMEM((doc_rows, features), f32),
            pltpu.VMEM((per_group, pairs, 2, chunk, features), f32),
            pltpu.VMEM((per_group, pairs, chunk, features), bf16),
            pltpu.VMEM((per_group, pairs, chunk, features), bf16),
            pltpu.VMEM((per_group, depth, chunk, features), bf16),
            pltpu.VMEM((per_group, depth, chunk, features), bf16),
            pltpu.VMEM((per_group, depth - 1, chunk, features), bf16),
            pltpu.VMEM((per_group, depth - 1, chunk, features), bf16),
            pltpu.VMEM((per_group, 2, layer_rows, features), f32),
            pltpu.VMEM((per_group * layer_rows, features), bf16),
            pltpu.VMEM((per_group * layer_rows, features), bf16),
            pltpu.VMEM((doc_rows // 2, features), bf16),
            pltpu.VMEM((doc_rows // 2, features), bf16),
            pltpu.VMEM((4,) + biases.shape, f32),
            pltpu.VMEM((depth + 2,) + biases.shape, f32),
            dma((per_group,)),
            dma((per_group,)),
            dma((per_group,)),
            dma((per_group,)),
            dma((per_group, depth - 1)),
            dma((per_group, depth - 1)),
            dma((depth + 1,)),
            dma((depth + 1,)),
            dma((3,)),
            dma((3,)),
        ],
        compiler_params=pltpu.CompilerParams(
            collective_id=0, has_side_effects=True, vmem_limit_bytes=56 * MIB
        ),
        cost_estimate=pl.CostEstimate(
            flops=flops, bytes_accessed=8 * MIB, transcendentals=0
        ),
        name="window",
    )(docs, docs_t, layers, biases, targets)


def outer_kernel(query_ref, grad_ref, out_ref):
    out_ref[...] = jnp.dot(
        query_ref[...], grad_ref[0], preferred_element_type=jnp.float32
    ).astype(out_ref.dtype)


def outer(queries, grads):
    rows, count, features = grads.shape
    return pl.pallas_call(
        outer_kernel,
        grid=(rows,),
        out_shape=jax.ShapeDtypeStruct((queries.shape[1], rows * features), jnp.bfloat16),
        in_specs=[
            pl.BlockSpec((queries.shape[1], count), lambda r: (0, 0)),
            pl.BlockSpec((1, count, features), lambda r: (r, 0, 0)),
        ],
        out_specs=pl.BlockSpec((queries.shape[1], features), lambda r: (0, r)),
        compiler_params=pltpu.CompilerParams(vmem_limit_bytes=32 * MIB),
        name="outer",
    )(queries.T, grads)


def fused_shards(queries, hyper_weight, hyper_bias, documents, teacher):
    features = queries.shape[1]
    lane_count = lax.axis_size("lane")
    per_group = queries.shape[0] // 2
    layer_rows = hyper_weight.shape[1] // features
    depth = lane_count // 4
    scale = features ** (-0.5)
    group = lax.axis_index("group")
    swap = [(0, 1), (1, 0)]
    other_docs = lax.ppermute(documents, "group", swap)
    other_teacher = lax.ppermute(teacher, "group", swap)
    generated = jnp.dot(queries, hyper_weight, preferred_element_type=jnp.float32).astype(
        jnp.bfloat16
    )
    bias_part = jnp.dot(queries, hyper_bias, preferred_element_type=jnp.float32).astype(
        jnp.bfloat16
    )
    rows = per_group * layer_rows
    extra = jnp.pad(
        bias_part.reshape(2, 1, rows), ((0, 0), (0, 15), (0, features - rows))
    )
    packed = jnp.concatenate([generated.reshape(2, rows, features), extra], axis=1)
    mine = lax.dynamic_index_in_dim(packed, group, 0, keepdims=False)
    theirs = lax.dynamic_index_in_dim(packed, 1 - group, 0, keepdims=False)
    got = lax.ppermute(theirs, "group", swap)
    pieces = jnp.where(group == 0, jnp.stack([mine, got]), jnp.stack([got, mine]))
    gathered = lax.all_gather(pieces, "lane", axis=0)
    layers = (
        gathered[:, :, :rows]
        .reshape(lane_count, 2, per_group, layer_rows, features)
        .transpose(2, 1, 0, 3, 4)
        .reshape(per_group, features, features)
    )
    biases = (
        gathered[:, :, rows, :rows]
        .reshape(lane_count, 2, per_group, layer_rows)
        .transpose(2, 1, 0, 3)
        .reshape(per_group, features)
        .astype(jnp.float32)
    )
    biases = jnp.pad(biases, ((0, -per_group % 8), (0, 0)))
    docs = jnp.concatenate([documents, other_docs])
    docs_t = (
        docs.T.reshape(2, lane_count, layer_rows, docs.shape[0])
        .transpose(1, 0, 2, 3)
        .reshape(features, docs.shape[0])
    )
    targets = lax.dynamic_slice_in_dim(
        jnp.concatenate([teacher, other_teacher]), group * per_group, per_group, 1
    ).astype(jnp.float32)
    doc_grad, grads, bias_sums = window(
        docs, docs_t, layers, biases, targets, depth, layer_rows, scale
    )
    grads = grads.reshape(2 * per_group, layer_rows, features).transpose(1, 0, 2)
    weight_grad = outer(queries, grads)
    first = (group * lane_count + lax.axis_index("lane")) * layer_rows
    bias_rows = bias_sums[:, :per_group].reshape(2 * per_group, features)
    gen_bias_grad = lax.dynamic_slice_in_dim(bias_rows, first, layer_rows, 1).astype(jnp.bfloat16)
    bias_grad = lax.dot_general(
        queries, gen_bias_grad, (((0,), (0,)), ((), ())), preferred_element_type=jnp.float32
    ).astype(jnp.bfloat16)
    return (doc_grad, weight_grad, bias_grad)


def shards(queries, hyper_weight, hyper_bias, documents, teacher):
    features = queries.shape[1]
    group_count = lax.axis_size("group")
    lane_count = lax.axis_size("lane")
    per_group = queries.shape[0] // group_count
    layer_rows = hyper_weight.shape[1] // features
    pool_scale = features ** (-0.5)
    generated = (
        jnp.dot(queries, hyper_weight, preferred_element_type=jnp.float32)
        .astype(jnp.bfloat16)
        .reshape(-1, layer_rows, features)
    )
    bias_part = jnp.dot(queries, hyper_bias, preferred_element_type=jnp.float32).astype(
        jnp.bfloat16
    )
    doc_rows, targets = (
        lax.all_gather(documents, "group", axis=0, tiled=True),
        lax.all_gather(teacher, "group", axis=0, tiled=True),
    )
    first_query = lax.axis_index("group") * per_group
    targets = lax.dynamic_slice_in_dim(targets, first_query, per_group, 1).astype(jnp.float32)
    pieces, bias_pieces = (
        lax.all_to_all(generated, "group", split_axis=0, concat_axis=1, tiled=True),
        lax.all_to_all(bias_part, "group", split_axis=0, concat_axis=1, tiled=True),
    )
    pieces, bias_pieces = (
        lax.all_gather(pieces, "lane", axis=1, tiled=True),
        lax.all_gather(bias_pieces, "lane", axis=1, tiled=True),
    )
    layers = (
        pieces.reshape(per_group, lane_count, group_count, layer_rows, features)
        .transpose(0, 2, 1, 3, 4)
        .reshape(per_group, features, features)
    )
    biases = (
        bias_pieces.reshape(per_group, lane_count, group_count, layer_rows)
        .transpose(0, 2, 1, 3)
        .reshape(per_group, features)
    )
    layer_list = []
    bias_list = []
    doc_total = None
    for number in range(per_group):
        preact = jnp.dot(doc_rows, layers[number], preferred_element_type=jnp.float32) + biases[
            number
        ].astype(jnp.float32)
        scores = jnp.sum(jnp.maximum(preact, 0.0), axis=1) * pool_scale
        errors = scores - targets[:, number]
        back_pre = jnp.where(preact > 0, errors[:, None] * pool_scale, 0.0).astype(jnp.bfloat16)
        layer_list.append(
            lax.dot_general(
                doc_rows, back_pre, (((0,), (0,)), ((), ())), preferred_element_type=jnp.float32
            )
        )
        bias_list.append(jnp.sum(back_pre.astype(jnp.float32), axis=0))
        doc_term = lax.dot_general(
            back_pre, layers[number], (((1,), (1,)), ((), ())), preferred_element_type=jnp.float32
        )
        doc_total = doc_term if doc_total is None else doc_total + doc_term
    layer_grads = jnp.stack(layer_list)
    bias_grads = jnp.stack(bias_list)
    ordered = (
        layer_grads.reshape(per_group, group_count, lane_count, layer_rows, features)
        .transpose(0, 2, 1, 3, 4)
        .reshape(per_group, features, features)
    )
    bias_ordered = (
        bias_grads.reshape(per_group, group_count, lane_count, layer_rows)
        .transpose(0, 2, 1, 3)
        .reshape(per_group, features)
    )
    grads, bias_sums = (
        lax.psum_scatter(ordered, "lane", scatter_dimension=1, tiled=True),
        lax.psum_scatter(bias_ordered, "lane", scatter_dimension=1, tiled=True),
    )
    grads, bias_sums = (
        lax.all_to_all(
            grads.astype(jnp.bfloat16), "group", split_axis=1, concat_axis=0, tiled=True
        ).astype(grads.dtype),
        lax.all_to_all(
            bias_sums.astype(jnp.bfloat16), "group", split_axis=1, concat_axis=0, tiled=True
        ).astype(bias_sums.dtype),
    )
    gen_grad = grads.astype(jnp.bfloat16).reshape(-1, layer_rows * features)
    gen_bias_grad = bias_sums.astype(jnp.bfloat16)
    weight_grad = lax.dot_general(
        queries, gen_grad, (((0,), (0,)), ((), ())), preferred_element_type=jnp.float32
    ).astype(jnp.bfloat16)
    bias_grad = lax.dot_general(
        queries, gen_bias_grad, (((0,), (0,)), ((), ())), preferred_element_type=jnp.float32
    ).astype(jnp.bfloat16)
    doc_grad = lax.psum_scatter(
        doc_total.astype(jnp.bfloat16), "group", scatter_dimension=0, tiled=True
    )
    return (doc_grad, weight_grad, bias_grad)


def solution(mesh):
    placed = (
        P(),
        P(None, ("group", "lane")),
        P(None, ("group", "lane")),
        P(("group", "lane"), None),
        P(("group", "lane"), None),
    )
    groups, lanes = mesh.shape["group"], mesh.shape["lane"]

    def body(queries, hyper_weight, hyper_bias, documents, teacher):
        layer_rows = hyper_weight.shape[1] // queries.shape[1]
        fits = groups == 2 and lanes in (8, 16) and layer_rows % 8 == 0
        fits = fits and documents.shape[0] % 32 == 0 and queries.shape[0] % 4 == 0
        form = fused_shards if fits else shards
        return form(queries, hyper_weight, hyper_bias, documents, teacher)

    return jax.shard_map(
        body,
        mesh=mesh,
        in_specs=placed,
        out_specs=(
            P(("group", "lane"), None),
            P(None, ("group", "lane")),
            P(None, ("group", "lane")),
        ),
        check_vma=False,
    )
```
